32 devices in a mesh: feat: 8 (over z, x), ex: 4 (over y, core).
Axes of the slice: x: 2, y: 2, z: 4, core: 2. Of those that a mesh axis runs over, the one named last changes fastest.
Arguments:
- grads: bfloat16 [256, 1048576], P('ex', 'feat'), may hold values from -6 to 6
- first_factor: bfloat16 [1024, 1024, 64], P('feat'), may hold values from -0.1875 to 0.1875
- second_factor: bfloat16 [64, 1024, 128], P('feat'), may hold values from -0.1875 to 0.1875
- picks: int32 [8, 8], replicated, may hold values from 0 to 255
Outputs:
- sketch: float32 [256, 8192], P('ex', 'feat')
- coverage: float32 [8, 256], P(None, 'ex')
The draws below stay inside these ranges and needn't reach their ends.
All inputs are finite; a program needn't handle non-finite values.
Results may differ from the reference program's by a relative error of at most 0.003.
Values may be sent and summed in bfloat16 or wider, within the bound.
No kernel may reach another device: no remote copies, remote signals or barrier semaphores. Data moves between devices by JAX's collectives and lax.ppermute only.
A program may use at most 128 MiB of HBM per device.

```python
import jax
import jax.numpy as jnp
from jax import lax

NB = 1024
BS = 1024
R1 = 64
R2 = 128
ROUNDS = 8
PICKS = 8
FEATS = 1048576
SKETCH = 8192
EXAMPLES = 256


def draw_grads(key, part):
    key = jax.random.fold_in(key, 11)
    key_member, key_level, key_proto, key_noise = jax.random.split(key, 4)
    prototypes_count = 64
    member = jax.random.randint(key_member, (EXAMPLES,), 0, prototypes_count)
    levels = jax.random.uniform(key_level, (prototypes_count, 1), jnp.float32, 0.5, 1.5)
    protos = jax.random.normal(key_proto, (prototypes_count, FEATS), jnp.float32)
    noise = 0.1 * jax.random.normal(key_noise, (EXAMPLES, FEATS), jnp.float32)
    rows = jnp.take(protos * levels, member, axis=0) + noise
    return jnp.clip(rows, -6.0, 6.0).astype(jnp.bfloat16)


def plant(array, own_key, smallest, largest):
    shape = array.shape
    index_at = [jax.random.randint(jax.random.fold_in(own_key, axis), (), 0, shape[axis]) for axis in range(len(shape))]
    array = array.at[tuple(index_at)].set(smallest)
    longest = shape.index(max(shape))
    index_at[longest] = (index_at[longest] + 1) % shape[longest]
    return array.at[tuple(index_at)].set(largest)


def steps_of(key, dims, pieces, low, largest):
    def one(axis_at, parts):
        heights = jax.random.uniform(jax.random.fold_in(jax.random.fold_in(key, 6), axis_at), (parts,), jnp.float32, low / len(pieces), largest / len(pieces))
        return jnp.repeat(jnp.exp(heights), dims[axis_at] // parts).reshape((-1,) + (1,) * (len(dims) - axis_at - 1))

    gain = one(*pieces[0])
    for cut in pieces[1:]:
        gain = gain * one(*cut)
    return gain


def centred(own_key, extent, width, most, pieces=(), held_as=jnp.bfloat16):
    drawn = width * jax.random.normal(own_key, extent, jnp.float32)
    if pieces:
        drawn = drawn * steps_of(own_key, extent, pieces, -0.22, 0.18)
    return jnp.clip(drawn, -most, most).astype(held_as)


def setup_inputs(seed: int = 0) -> dict:
    streams_of = jax.random.split(jax.random.key(seed), 5)
    grads = draw_grads(jax.random.fold_in(streams_of[4], 71), 0)
    first_factor = centred(streams_of[1], (NB, BS, R1), BS ** -0.5, 0.1875, ((0, 8),))
    second_factor = centred(streams_of[2], (R1, NB, R2), NB ** -0.5, 0.1875, ((0, 8),))
    picks = plant(jax.random.randint(streams_of[3], (ROUNDS, PICKS), 0, EXAMPLES), jax.random.fold_in(streams_of[3], 1), 0, EXAMPLES - 1).astype(jnp.int32)
    return {"grads": grads, "first_factor": first_factor, "second_factor": second_factor, "picks": picks}


def reference(grads, first_factor, second_factor, picks):
    blocks = grads.reshape(EXAMPLES, NB, BS)

    def first_block(b):
        rows = lax.dynamic_index_in_dim(blocks, b, 1, keepdims=False)
        weight = lax.dynamic_index_in_dim(first_factor, b, 0, keepdims=False)
        return jnp.dot(rows, weight, preferred_element_type=jnp.float32).astype(jnp.bfloat16)

    inner = lax.map(first_block, jnp.arange(NB, dtype=jnp.int32))

    def second_group(k):
        cols = lax.dynamic_index_in_dim(inner, k, 2, keepdims=False)
        weight = lax.dynamic_index_in_dim(second_factor, k, 0, keepdims=False)
        return jnp.dot(cols.T, weight, preferred_element_type=jnp.float32)

    groups = lax.map(second_group, jnp.arange(R1, dtype=jnp.int32))
    sketch = jnp.transpose(groups, (1, 0, 2)).reshape(EXAMPLES, SKETCH)

    def one_center(index):
        center = lax.dynamic_index_in_dim(sketch, index, 0, keepdims=False)
        diff = sketch - center[None, :]
        return jnp.sum(diff * diff, axis=1) / SKETCH

    rows_out = []
    running = None
    for r in range(ROUNDS):
        dists = lax.map(one_center, picks[r])
        nearest = jnp.min(dists, axis=0)
        running = nearest if running is None else jnp.minimum(running, nearest)
        rows_out.append(running)
    return sketch, jnp.stack(rows_out, axis=0)
```

```python
import functools

import jax
import jax.numpy as jnp
from jax import lax
from jax.experimental import pallas as pl
from jax.experimental.pallas import tpu as pltpu
from jax.sharding import PartitionSpec as P

F32 = jnp.float32
BF16 = jnp.bfloat16
VMEM_LIMIT = 48 * 1024 * 1024
NT = (((1,), (1,)), ((), ()))
NN = (((1,), (0,)), ((), ()))


def params(**kw):
    return pltpu.CompilerParams(vmem_limit_bytes=VMEM_LIMIT, **kw)


def first_kernel(step_blocks, half, flush, g0, g1, w0, w1, out, acc):
    s = pl.program_id(0)
    groups, size = w0.shape[1], w0.shape[2]
    for t in range(step_blocks):
        cols = slice(t * size, (t + 1) * size)
        low = lax.dot_general(w0[t], g0[:, cols], NT, preferred_element_type=F32)
        high = lax.dot_general(w1[t], g1[:, cols], NT, preferred_element_type=F32)
        row = s * step_blocks + t
        acc[pl.ds(row, groups, stride=half), :] = jnp.concatenate([low, high], axis=1)

    steps = flush // step_blocks

    @pl.when(s % steps == steps - 1)
    def _():
        start = pl.multiple_of((s // steps) * flush, flush)
        for k in range(groups):
            out[k, pl.ds(start, flush), :] = acc[pl.ds(k * half + start, flush), :].astype(BF16)


def first_products(grads, factor, start, count):
    rows = grads.shape[0]
    _, groups, size = factor.shape
    half = count // 2
    step_blocks = min(4, half)
    flush = min(16, half)
    low, high = start // step_blocks, (start + half) // step_blocks
    g_spec = lambda first: pl.BlockSpec((rows, step_blocks * size), lambda s, first=first: (0, first + s))
    w_spec = lambda first: pl.BlockSpec((step_blocks, groups, size), lambda s, first=first: (first + s, 0, 0))
    return pl.pallas_call(
        functools.partial(first_kernel, step_blocks, half, flush),
        grid=(half // step_blocks,),
        in_specs=[g_spec(low), g_spec(high), w_spec(low), w_spec(high)],
        out_specs=pl.BlockSpec((groups, half, 2 * rows), lambda s: (0, 0, 0)),
        out_shape=jax.ShapeDtypeStruct((groups, half, 2 * rows), BF16),
        scratch_shapes=[pltpu.VMEM((groups * half, 2 * rows), F32)],
        compiler_params=params(dimension_semantics=("arbitrary",)),
        cost_estimate=pl.CostEstimate(
            flops=2 * count * rows * groups * size,
            bytes_accessed=2 * count * size * (rows + groups),
            transcendentals=0,
        ),
        name="first_products",
    )(grads, grads, factor, factor)


def turn_kernel(halves, second, *outs):
    groups, sources, _, width = second.shape
    for k in range(groups):
        start = 0
        for half, out in zip(halves, outs):
            for h in range(2):
                rows = second[k, :, start + h * half : start + (h + 1) * half, :]
                rows = rows.reshape(sources * half, width)
                out[k, h * width : (h + 1) * width, :] = rows.T
            start += 2 * half


def turned(second, sources, halves):
    groups, total, width = second.shape
    second = second.reshape(groups, sources, total // sources, width)
    return pl.pallas_call(
        functools.partial(turn_kernel, halves),
        out_shape=[jax.ShapeDtypeStruct((groups, 2 * width, sources * half), BF16) for half in halves],
        compiler_params=params(),
        name="turned_factor",
    )(second)


def second_kernel(chunks, *refs):
    base, picks, *rest = refs
    turned_refs, pieces, (sketch, fetched, held) = rest[:chunks], rest[chunks : 2 * chunks], rest[2 * chunks :]
    groups, both, _ = turned_refs[0].shape
    width, rows = both // 2, sketch.shape[0]
    slots = fetched.shape[1]
    if groups < slots:
        held[...] = jnp.zeros_like(held)
    for k in range(groups):
        total = None
        for a, x in zip(turned_refs, pieces):
            right = x[:, k].reshape(a.shape[2], 2 * rows)
            part = lax.dot_general(a[k], right, NN, preferred_element_type=F32)
            total = part if total is None else total + part
        mapped = (total[:width, :rows] + total[width:, rows:]).T
        sketch[:, k * width : (k + 1) * width] = mapped
        held[pl.ds(k, rows, stride=slots), :] = mapped
    rounds, each = picks.shape
    for r in range(rounds):
        for p in range(each):
            at = picks[r, p] - base[0]
            mine = (at >= 0) & (at < rows)
            start = pl.multiple_of(jnp.clip(at, 0, rows - 1) * slots, slots)
            fetched[r * each + p] = jnp.where(mine, held[pl.ds(start, slots), :], 0.0)


def second_products(base, picks, turned_factors, pieces, rows):
    chunks = len(pieces)
    groups, both, _ = turned_factors[0].shape
    width = both // 2
    slots = -(-groups // 8) * 8
    smem = pl.BlockSpec(memory_space=pltpu.SMEM)
    vmem = pl.BlockSpec(memory_space=pltpu.VMEM)
    return pl.pallas_call(
        functools.partial(second_kernel, chunks),
        in_specs=[smem, smem] + [vmem] * (2 * chunks),
        out_specs=[vmem, vmem],
        out_shape=[
            jax.ShapeDtypeStruct((rows, groups * width), F32),
            jax.ShapeDtypeStruct((picks.size, slots, width), F32),
        ],
        scratch_shapes=[pltpu.VMEM((rows * slots, width), F32)],
        compiler_params=params(),
        name="second_products",
    )(base, picks, *turned_factors, *pieces)


def distance_kernel(sketch, *refs):
    *fetched, out, total = refs
    rows, dims = sketch.shape
    count, _, width = total.shape
    center = fetched[0][...]
    for other in fetched[1:]:
        center = center + other[...]
    total[...] = center
    lane = lax.broadcasted_iota(jnp.int32, (rows, 128), 1)

    def one(p, sums):
        acc = None
        for t in range(dims // width):
            diff = sketch[:, t * width : (t + 1) * width] - total[p, t : t + 1, :]
            acc = diff * diff if acc is None else acc + diff * diff
        return jnp.where(lane == p, jnp.sum(acc, axis=1, keepdims=True), sums)

    sums = lax.fori_loop(0, count, one, jnp.zeros((rows, 128), F32))
    half = count // 2
    by_pick = sums.T
    out[...] = jnp.concatenate([by_pick[:half], by_pick[half:count]], axis=1)


def distances(sketch, fetched):
    vmem = pl.BlockSpec(memory_space=pltpu.VMEM)
    count = fetched[0].shape[0]
    return pl.pallas_call(
        distance_kernel,
        in_specs=[vmem] * (1 + len(fetched)),
        out_specs=vmem,
        out_shape=jax.ShapeDtypeStruct((count // 2, 2 * sketch.shape[0]), F32),
        scratch_shapes=[pltpu.VMEM(fetched[0].shape, F32)],
        compiler_params=params(),
        name="distances",
    )(sketch, *fetched)


def nearest_kernel(sketch_size, each, parts, out):
    total = parts[0]
    for i in range(1, parts.shape[0]):
        total = total + parts[i]
    total = total / sketch_size
    half, rows = out.shape[0] // 2, out.shape[1]
    near = [jnp.min(total[r * each : (r + 1) * each, :], axis=0, keepdims=True) for r in range(half)]
    running = None
    for r in range(2 * half):
        row = near[r % half][:, (r // half) * rows : (r // half + 1) * rows]
        running = row if running is None else jnp.minimum(running, row)
        out[r : r + 1, :] = running


def nearest(parts, sketch_size, rounds):
    vmem = pl.BlockSpec(memory_space=pltpu.VMEM)
    each = 2 * parts.shape[1] // rounds
    return pl.pallas_call(
        functools.partial(nearest_kernel, sketch_size, each),
        in_specs=[vmem],
        out_specs=vmem,
        out_shape=jax.ShapeDtypeStruct((rounds, parts.shape[2] // 2), F32),
        compiler_params=params(),
        name="nearest",
    )(parts)


def per_device(chunks, feat, ex, grads, first_factor, second_factor, picks):
    rows = grads.shape[0]
    local_blocks = first_factor.shape[0]
    groups, _, width = second_factor.shape
    factor = jnp.swapaxes(first_factor, 1, 2)
    pieces, start = [], 0
    for count in chunks:
        inner = first_products(grads, factor, start, count)
        piece = lax.all_to_all(inner, "feat", split_axis=0, concat_axis=0, tiled=True)
        pieces.append(piece.reshape(feat, groups, count // 2, 2 * rows))
        start += count
    turned_factors = turned(second_factor, feat, [count // 2 for count in chunks])
    base = (lax.axis_index("ex") * rows).astype(jnp.int32).reshape(1)
    sketch, fetched = second_products(base, picks, turned_factors, pieces, rows)
    step = 1
    parts = [fetched]
    while step < ex:
        parts = parts + [lax.ppermute(x, "ex", [(i, i ^ step) for i in range(ex)]) for x in parts]
        step *= 2
    part = distances(sketch, parts)
    spread = jnp.broadcast_to(part[None], (feat,) + part.shape)
    gathered = lax.all_to_all(spread, "feat", split_axis=0, concat_axis=0, tiled=True)
    coverage = nearest(gathered, feat * groups * width, picks.shape[0])
    return (sketch, coverage)


def solution(mesh):
    feat, ex = mesh.shape["feat"], mesh.shape["ex"]
    in_specs = (P("ex", "feat"), P("feat", None, None), P("feat", None, None), P())
    out_specs = (P("ex", "feat"), P(None, "ex"))

    def run(grads, first_factor, second_factor, picks):
        blocks = first_factor.shape[0] // feat
        chunks = [blocks]
        return jax.shard_map(
            functools.partial(per_device, chunks, feat, ex),
            mesh=mesh,
            in_specs=in_specs,
            out_specs=out_specs,
            check_vma=False,
        )(grads, first_factor, second_factor, picks)

    return run
```

```python
import functools

import jax
import jax.numpy as jnp
from jax import lax
from jax.experimental import pallas as pl
from jax.experimental.pallas import tpu as pltpu
from jax.sharding import PartitionSpec as P

F32 = jnp.float32
BF16 = jnp.bfloat16
MIB = 1024 * 1024
NT = (((1,), (1,)), ((), ()))
NN = (((1,), (0,)), ((), ()))


def params(mib=8):
    return pltpu.CompilerParams(vmem_limit_bytes=mib * MIB)


def first_kernel(feat, start, half, step, flush, *refs):
    grads, factor, *outs, g_buf, w_buf, acc, sems = refs
    _, groups, size = factor.shape
    kept = groups // feat
    steps = half // step
    split = len(outs) > 1
    me = lax.axis_index("feat") if split else 0

    def copies(i):
        for h in range(2):
            block = start + h * half + i * step
            yield pltpu.make_async_copy(
                grads.at[:, pl.ds(block * size, step * size)], g_buf.at[h, i], sems.at[h, i, 0]
            )
            yield pltpu.make_async_copy(factor.at[pl.ds(block, step)], w_buf.at[h, i], sems.at[h, i, 1])

    for i in range(steps):
        for copy in copies(i):
            copy.start()
    for i in range(steps):
        for copy in copies(i):
            copy.wait()
        for t in range(step):
            cols = slice(t * size, (t + 1) * size)
            low = lax.dot_general(w_buf[0, i, t], g_buf[0, i, :, cols], NT, preferred_element_type=F32)
            high = lax.dot_general(w_buf[1, i, t], g_buf[1, i, :, cols], NT, preferred_element_type=F32)
            acc[pl.ds(i * step + t, groups, stride=half), :] = jnp.concatenate([low, high], axis=1)
        if (i + 1) * step % flush == 0:
            done = (i + 1) * step - flush
            for d in range(feat):
                first = (me ^ d) * (kept * half)
                for q in range(kept):
                    at = pl.multiple_of(first + q * half + done, 8)
                    rows = acc[pl.ds(at, flush), :].astype(BF16)
                    if split:
                        outs[d][q, done : done + flush, :] = rows
                    else:
                        outs[0][d * kept + q, done : done + flush, :] = rows


def first_products(grads, factor, feat, start, count, split):
    rows = grads.shape[0]
    _, groups, size = factor.shape
    kept = groups // feat
    half = count // 2
    step, flush = min(4, half), min(16, half)
    steps = half // step
    lanes = 2 * rows
    if split:
        out_shape = [jax.ShapeDtypeStruct((kept, half, lanes), BF16)] * feat
    else:
        out_shape = [jax.ShapeDtypeStruct((groups, half, lanes), BF16)]
    vmem = pl.BlockSpec(memory_space=pltpu.VMEM)
    hbm = pl.BlockSpec(memory_space=pl.ANY)
    return pl.pallas_call(
        functools.partial(first_kernel, feat, start, half, step, flush),
        in_specs=[hbm, hbm],
        out_specs=[vmem] * len(out_shape),
        out_shape=out_shape,
        scratch_shapes=[
            pltpu.VMEM((2, steps, rows, step * size), BF16),
            pltpu.VMEM((2, steps, step, groups, size), BF16),
            pltpu.VMEM((groups * half, lanes), F32),
            pltpu.SemaphoreType.DMA((2, steps, 2)),
        ],
        compiler_params=params(48),
        cost_estimate=pl.CostEstimate(
            flops=2 * count * rows * groups * size,
            bytes_accessed=2 * count * size * (rows + groups),
            transcendentals=0,
        ),
        name="first_products",
    )(grads, factor)


def turn_kernel(plan, local, second, *outs):
    me = lax.axis_index("feat")
    for (relative, sources, start, half), out in zip(plan, outs):
        for k in range(second.shape[0]):
            for h in range(2):
                rows = []
                for d in sources:
                    source = me ^ d if relative else d
                    at = source * local + start + h * half
                    rows.append(second[k, pl.ds(pl.multiple_of(at, 8) if relative else at, half), :])
                width = second.shape[2]
                out[k, h * width : (h + 1) * width, :] = jnp.concatenate(rows, axis=0).T


def turned(second, local, plan):
    groups, _, width = second.shape
    vmem = pl.BlockSpec(memory_space=pltpu.VMEM)
    return pl.pallas_call(
        functools.partial(turn_kernel, plan, local),
        in_specs=[vmem],
        out_specs=[vmem] * len(plan),
        out_shape=[
            jax.ShapeDtypeStruct((groups, 2 * width, len(sources) * half), BF16) for _, sources, _, half in plan
        ],
        compiler_params=params(),
        name="turned_factor",
    )(second)


def products(k, factors, pieces, rows):
    total = None
    for a, own in zip(factors, pieces):
        if len(own) == 1:
            groups = a.shape[0]
            own = [own[0].at[pl.ds(s * groups, groups)] for s in range(own[0].shape[0] // groups)]
        right = jnp.concatenate([x[k] for x in own], axis=0)
        part = lax.dot_general(a[k], right, NN, preferred_element_type=F32)
        total = part if total is None else total + part
    width = total.shape[0] // 2
    return (total[:width, :rows] + total[width:, rows:]).T


def split_refs(counts, refs):
    refs = list(refs)
    factors = [refs.pop(0) for _ in counts]
    pieces = [[refs.pop(0) for _ in range(n)] for n in counts]
    return factors, pieces, refs


def early_kernel(counts, *refs):
    factors, pieces, (out,) = split_refs(counts, refs)
    groups, both, _ = factors[0].shape
    width = both // 2
    for k in range(groups):
        out[:, k * width : (k + 1) * width] = products(k, factors, pieces, out.shape[0])


def early_products(factors, pieces, rows):
    groups, both, _ = factors[0].shape
    vmem = pl.BlockSpec(memory_space=pltpu.VMEM)
    counts = [len(own) for own in pieces]
    return pl.pallas_call(
        functools.partial(early_kernel, counts),
        in_specs=[vmem] * (len(counts) + sum(counts)),
        out_specs=vmem,
        out_shape=jax.ShapeDtypeStruct((rows, groups * both // 2), F32),
        compiler_params=params(),
        name="early_products",
    )(*factors, *[x for own in pieces for x in own])


def late_kernel(counts, picks, early, *refs):
    factors, pieces, (sketch, mine, other, held) = split_refs(counts, refs)
    groups, both, _ = factors[0].shape
    width, rows = both // 2, sketch.shape[0]
    slots = mine.shape[1]
    if groups < slots:
        held[...] = jnp.zeros_like(held)
    for k in range(groups):
        cols = slice(k * width, (k + 1) * width)
        mapped = early[:, cols] + products(k, factors, pieces, rows)
        sketch[:, cols] = mapped
        held[pl.ds(k, rows, stride=slots), :] = mapped
    rounds, each = picks.shape
    place = lax.axis_index("ex")
    base, core = place * rows, place % 2
    half = rounds // 2
    for r in range(half):
        for p in range(each):
            for out, side in ((mine, core), (other, 1 - core)):
                at = picks[side * half + r, p] - base
                held_here = (at >= 0) & (at < rows)
                start = pl.multiple_of(jnp.clip(at, 0, rows - 1) * slots, slots)
                out[r * each + p] = jnp.where(held_here, held[pl.ds(start, slots), :], 0.0)


def late_products(picks, early, factors, pieces):
    rows = early.shape[0]
    groups, both, _ = factors[0].shape
    width = both // 2
    slots = -(-groups // 8) * 8
    smem = pl.BlockSpec(memory_space=pltpu.SMEM)
    vmem = pl.BlockSpec(memory_space=pltpu.VMEM)
    counts = [len(own) for own in pieces]
    fetched = jax.ShapeDtypeStruct((picks.size // 2, slots, width), F32)
    return pl.pallas_call(
        functools.partial(late_kernel, counts),
        in_specs=[smem] + [vmem] * (1 + len(counts) + sum(counts)),
        out_specs=[vmem] * 3,
        out_shape=[jax.ShapeDtypeStruct(early.shape, F32), fetched, fetched],
        scratch_shapes=[pltpu.VMEM((rows * slots, width), F32)],
        compiler_params=params(),
        name="late_products",
    )(picks, early, *factors, *[x for own in pieces for x in own])


def distance_kernel(unroll, sketch, first, second, *refs):
    *before, out, center = refs
    rows, dims = sketch.shape
    count, _, width = center.shape
    center[...] = first[...] + second[...]
    lane = lax.broadcasted_iota(jnp.int32, (8, 128), 1)

    def some(i, sums):
        sums = list(sums)
        for g in range(rows // 8):
            block = [sketch[g * 8 : (g + 1) * 8, t * width : (t + 1) * width] for t in range(dims // width)]
            for u in range(unroll):
                p = i * unroll + u
                acc = None
                for t, own in enumerate(block):
                    diff = own - center[p, t : t + 1, :]
                    acc = diff * diff if acc is None else acc + diff * diff
                sums[g] = jnp.where(lane == p, jnp.sum(acc, axis=1, keepdims=True), sums[g])
        return tuple(sums)

    zeros = tuple(jnp.zeros((8, 128), F32) for _ in range(rows // 8))
    sums = lax.fori_loop(0, count // unroll, some, zeros)
    by_pick = jnp.concatenate(sums, axis=0).T[:count]
    if before:
        by_pick = jnp.concatenate([before[0][...], by_pick], axis=1)
    out[...] = by_pick


def distances(sketch, first, second, before=()):
    vmem = pl.BlockSpec(memory_space=pltpu.VMEM)
    count, rows = first.shape[0], sketch.shape[0]
    return pl.pallas_call(
        functools.partial(distance_kernel, 4),
        in_specs=[vmem] * (3 + len(before)),
        out_specs=vmem,
        out_shape=jax.ShapeDtypeStruct((count, rows * (1 + len(before))), F32),
        scratch_shapes=[pltpu.VMEM(first.shape, F32)],
        compiler_params=params(),
        name="distances",
    )(sketch, first, second, *before)


def nearest_kernel(sketch_size, each, parts, out):
    total = parts[0]
    for i in range(1, parts.shape[0]):
        total = total + parts[i]
    total = total / sketch_size
    half, rows = out.shape[0] // 2, out.shape[1]
    core = lax.axis_index("ex") % 2
    near = [jnp.min(total[r * each : (r + 1) * each, :], axis=0, keepdims=True) for r in range(half)]
    running = None
    for r in range(2 * half):
        own, other = near[r % half][:, :rows], near[r % half][:, rows:]
        row = jnp.where(core == r // half, own, other)
        running = row if running is None else jnp.minimum(running, row)
        out[r : r + 1, :] = running


def nearest(parts, sketch_size, rounds):
    vmem = pl.BlockSpec(memory_space=pltpu.VMEM)
    each = 2 * parts.shape[1] // rounds
    return pl.pallas_call(
        functools.partial(nearest_kernel, sketch_size, each),
        in_specs=[vmem],
        out_specs=vmem,
        out_shape=jax.ShapeDtypeStruct((rounds, parts.shape[2] // 2), F32),
        compiler_params=params(),
        name="nearest",
    )(parts)


def swap(x, axis, size, step):
    return lax.ppermute(x, axis, [(i, i ^ step) for i in range(size)])


def per_device(feat, ex, grads, first_factor, second_factor, picks):
    rows = grads.shape[0]
    local = first_factor.shape[0]
    groups, _, width = second_factor.shape
    near = feat // 2
    factor = jnp.swapaxes(first_factor, 1, 2)
    first_count = local // 2 if local % 64 == 0 else 0
    plan, pieces = [], []
    if first_count:
        (inner,) = first_products(grads, factor, feat, 0, first_count, False)
        inner = lax.all_to_all(inner, "feat", split_axis=0, concat_axis=0, tiled=True)
        pieces.append([inner])
        plan.append((False, tuple(range(feat)), 0, first_count // 2))
    split = first_products(grads, factor, feat, first_count, local - first_count, True)
    far = [swap(x, "feat", feat, d) for d, x in enumerate(split) if d >= near]
    close = [x if d == 0 else swap(x, "feat", feat, d) for d, x in enumerate(split[:near])]
    pieces += [close, far]
    half = (local - first_count) // 2
    plan += [(True, tuple(range(near)), first_count, half), (True, tuple(range(near, feat)), first_count, half)]

    factors = turned(second_factor, local, plan)
    early = early_products(factors[:-1], pieces[:-1], rows)
    sketch, mine, other = late_products(picks, early, factors[-1:], pieces[-1:])

    chip = mine + swap(other, "ex", ex, 1)
    across = [chip]
    step = 2
    while step < ex:
        across = across + [swap(x, "ex", ex, step) for x in across]
        step *= 2
    across = [across[0], sum(across[1:])]
    part = distances(sketch, *across)
    part = distances(sketch, *[swap(x, "ex", ex, 1) for x in across], before=(part,))
    spread = jnp.broadcast_to(part[None], (feat,) + part.shape)
    gathered = lax.all_to_all(spread, "feat", split_axis=0, concat_axis=0, tiled=True)
    coverage = nearest(gathered, feat * groups * width, picks.shape[0])
    return (sketch, coverage)


def solution(mesh):
    feat, ex = mesh.shape["feat"], mesh.shape["ex"]
    in_specs = (P("ex", "feat"), P("feat", None, None), P("feat", None, None), P())
    out_specs = (P("ex", "feat"), P(None, "ex"))
    return jax.shard_map(
        functools.partial(per_device, feat, ex),
        mesh=mesh,
        in_specs=in_specs,
        out_specs=out_specs,
        check_vma=False,
    )
```

```python
import functools

import jax
import jax.numpy as jnp
from jax import lax
from jax.experimental import pallas as pl
from jax.experimental.pallas import tpu as pltpu
from jax.sharding import PartitionSpec as P

F32 = jnp.float32
BF16 = jnp.bfloat16
MIB = 1024 * 1024
NT = (((1,), (1,)), ((), ()))
NN = (((1,), (0,)), ((), ()))


def params(mib=8):
    return pltpu.CompilerParams(vmem_limit_bytes=mib * MIB)


def first_kernel(feat, start, half, step, flush, *refs):
    grads, factor, *outs, g_buf, w_buf, acc, sems = refs
    _, groups, size = factor.shape
    kept = groups // feat
    steps = half // step
    split = len(outs) > 1
    me = lax.axis_index("feat") if split else 0

    def copies(i):
        for h in range(2):
            block = start + h * half + i * step
            yield pltpu.make_async_copy(
                grads.at[:, pl.ds(block * size, step * size)], g_buf.at[h, i], sems.at[h, i, 0]
            )
            yield pltpu.make_async_copy(factor.at[pl.ds(block, step)], w_buf.at[h, i], sems.at[h, i, 1])

    for i in range(steps):
        for copy in copies(i):
            copy.start()
    for i in range(steps):
        for copy in copies(i):
            copy.wait()
        for t in range(step):
            cols = slice(t * size, (t + 1) * size)
            low = lax.dot_general(w_buf[0, i, t], g_buf[0, i, :, cols], NT, preferred_element_type=F32)
            high = lax.dot_general(w_buf[1, i, t], g_buf[1, i, :, cols], NT, preferred_element_type=F32)
            acc[pl.ds(i * step + t, groups, stride=half), :] = jnp.concatenate([low, high], axis=1)
        if (i + 1) * step % flush == 0:
            done = (i + 1) * step - flush
            for d in range(feat):
                first = (me ^ d) * (kept * half)
                for q in range(kept):
                    at = pl.multiple_of(first + q * half + done, 8)
                    rows = acc[pl.ds(at, flush), :].astype(BF16)
                    if split:
                        outs[d][q, done : done + flush, :] = rows
                    else:
                        outs[0][d * kept + q, done : done + flush, :] = rows


def first_products(grads, factor, feat, split, start, count):
    rows = grads.shape[0]
    _, groups, size = factor.shape
    kept = groups // feat
    half = count // 2
    step, flush = min(4, half), min(16, half)
    steps = half // step
    lanes = 2 * rows
    if split:
        out_shape = [jax.ShapeDtypeStruct((kept, half, lanes), BF16)] * feat
    else:
        out_shape = [jax.ShapeDtypeStruct((groups, half, lanes), BF16)]
    vmem = pl.BlockSpec(memory_space=pltpu.VMEM)
    hbm = pl.BlockSpec(memory_space=pl.ANY)
    return pl.pallas_call(
        functools.partial(first_kernel, feat, start, half, step, flush),
        in_specs=[hbm, hbm],
        out_specs=[vmem] * len(out_shape),
        out_shape=out_shape,
        scratch_shapes=[
            pltpu.VMEM((2, steps, rows, step * size), BF16),
            pltpu.VMEM((2, steps, step, groups, size), BF16),
            pltpu.VMEM((groups * half, lanes), F32),
            pltpu.SemaphoreType.DMA((2, steps, 2)),
        ],
        compiler_params=params(48),
        cost_estimate=pl.CostEstimate(
            flops=2 * count * rows * groups * size,
            bytes_accessed=2 * count * size * (rows + groups),
            transcendentals=0,
        ),
        name="first_products",
    )(grads, factor)


def turn_kernel(plan, local, second, *outs):
    me = lax.axis_index("feat")
    width = second.shape[2]
    for spans, out in zip(plan, outs):
        for k in range(second.shape[0]):
            for h in range(2):
                rows = []
                for relative, source, start, half in spans:
                    if relative:
                        at = pl.multiple_of((me ^ source) * local + start + h * half, 8)
                    else:
                        at = source * local + start + h * half
                    rows.append(second[k, pl.ds(at, half), :])
                out[k, h * width : (h + 1) * width, :] = jnp.concatenate(rows, axis=0).T


def turned(second, local, plan):
    groups, _, width = second.shape
    vmem = pl.BlockSpec(memory_space=pltpu.VMEM)
    return pl.pallas_call(
        functools.partial(turn_kernel, plan, local),
        in_specs=[vmem],
        out_specs=[vmem] * len(plan),
        out_shape=[
            jax.ShapeDtypeStruct((groups, 2 * width, sum(span[-1] for span in spans)), BF16) for spans in plan
        ],
        compiler_params=params(),
        name="turned_factor",
    )(second)


def products(k, factors, pieces, rows):
    total = None
    for a, own in zip(factors, pieces):
        groups = a.shape[0]
        right = jnp.concatenate([x[at + k] for x in own for at in range(0, x.shape[0], groups)], axis=0)
        part = lax.dot_general(a[k], right, NN, preferred_element_type=F32)
        total = part if total is None else total + part
    width = total.shape[0] // 2
    return (total[:width, :rows] + total[width:, rows:]).T


def split_refs(counts, refs):
    refs = list(refs)
    factors = [refs.pop(0) for _ in counts]
    pieces = [[refs.pop(0) for _ in range(n)] for n in counts]
    return factors, pieces, refs


def early_kernel(counts, *refs):
    factors, pieces, (out,) = split_refs(counts, refs)
    groups, both, _ = factors[0].shape
    width = both // 2
    for k in range(groups):
        out[:, k * width : (k + 1) * width] = products(k, factors, pieces, out.shape[0])


def early_products(factors, pieces, rows):
    groups, both, _ = factors[0].shape
    vmem = pl.BlockSpec(memory_space=pltpu.VMEM)
    counts = [len(own) for own in pieces]
    return pl.pallas_call(
        functools.partial(early_kernel, counts),
        in_specs=[vmem] * (len(counts) + sum(counts)),
        out_specs=vmem,
        out_shape=jax.ShapeDtypeStruct((rows, groups * both // 2), F32),
        compiler_params=params(),
        name="early_products",
    )(*factors, *[x for own in pieces for x in own])


def late_kernel(counts, picks, early, *refs):
    factors, pieces, (sketch, mine, other, held) = split_refs(counts, refs)
    groups, both, _ = factors[0].shape
    width, rows = both // 2, sketch.shape[0]
    slots = mine.shape[1]
    if groups < slots:
        held[...] = jnp.zeros_like(held)
    for k in range(groups):
        cols = slice(k * width, (k + 1) * width)
        mapped = early[:, cols] + products(k, factors, pieces, rows)
        sketch[:, cols] = mapped
        held[pl.ds(k, rows, stride=slots), :] = mapped
    rounds, each = picks.shape
    place = lax.axis_index("ex")
    base, core = place * rows, place % 2
    half = rounds // 2
    for r in range(half):
        for p in range(each):
            for out, side in ((mine, core), (other, 1 - core)):
                at = picks[side * half + r, p] - base
                held_here = (at >= 0) & (at < rows)
                start = pl.multiple_of(jnp.clip(at, 0, rows - 1) * slots, slots)
                out[r * each + p] = jnp.where(held_here, held[pl.ds(start, slots), :], 0.0)


def late_products(picks, early, factors, pieces):
    rows = early.shape[0]
    groups, both, _ = factors[0].shape
    width = both // 2
    slots = -(-groups // 8) * 8
    smem = pl.BlockSpec(memory_space=pltpu.SMEM)
    vmem = pl.BlockSpec(memory_space=pltpu.VMEM)
    counts = [len(own) for own in pieces]
    fetched = jax.ShapeDtypeStruct((picks.size // 2, slots, width), F32)
    return pl.pallas_call(
        functools.partial(late_kernel, counts),
        in_specs=[smem] + [vmem] * (1 + len(counts) + sum(counts)),
        out_specs=[vmem] * 3,
        out_shape=[jax.ShapeDtypeStruct(early.shape, F32), fetched, fetched],
        scratch_shapes=[pltpu.VMEM((rows * slots, width), F32)],
        compiler_params=params(),
        name="late_products",
    )(picks, early, *factors, *[x for own in pieces for x in own])


def distance_kernel(unroll, sketch, first, second, *refs):
    if len(refs) == 4:
        kept, out, center, sem = refs
        before = None
        copy = pltpu.make_async_copy(sketch, kept, sem)
        copy.start()
    else:
        before, out, center = refs
        copy = None
    rows, dims = sketch.shape
    count, _, width = center.shape
    center[...] = first[...] + second[...]
    lane = lax.broadcasted_iota(jnp.int32, (8, 128), 1)

    def some(i, sums):
        sums = list(sums)
        for g in range(rows // 8):
            block = [sketch[g * 8 : (g + 1) * 8, t * width : (t + 1) * width] for t in range(dims // width)]
            for u in range(unroll):
                p = i * unroll + u
                acc = None
                for t, own in enumerate(block):
                    diff = own - center[p, t : t + 1, :]
                    acc = diff * diff if acc is None else acc + diff * diff
                sums[g] = jnp.where(lane == p, jnp.sum(acc, axis=1, keepdims=True), sums[g])
        return tuple(sums)

    zeros = tuple(jnp.zeros((8, 128), F32) for _ in range(rows // 8))
    sums = lax.fori_loop(0, count // unroll, some, zeros)
    by_pick = jnp.concatenate(sums, axis=0).T[:count]
    if before is not None:
        by_pick = jnp.concatenate([before[...], by_pick], axis=1)
    out[...] = by_pick.astype(out.dtype)
    if copy is not None:
        copy.wait()


def distances(sketch, first, second, before=None):
    vmem = pl.BlockSpec(memory_space=pltpu.VMEM)
    hbm = pl.BlockSpec(memory_space=pl.ANY)
    count, rows = first.shape[0], sketch.shape[0]
    center = pltpu.VMEM(first.shape, F32)
    if before is None:
        return pl.pallas_call(
            functools.partial(distance_kernel, 4),
            in_specs=[vmem] * 3,
            out_specs=[hbm, vmem],
            out_shape=[jax.ShapeDtypeStruct(sketch.shape, F32), jax.ShapeDtypeStruct((count, rows), F32)],
            scratch_shapes=[center, pltpu.SemaphoreType.DMA],
            compiler_params=params(),
            name="distances",
        )(sketch, first, second)
    return pl.pallas_call(
        functools.partial(distance_kernel, 4),
        in_specs=[vmem] * 4,
        out_specs=vmem,
        out_shape=jax.ShapeDtypeStruct((count, 2 * rows), BF16),
        scratch_shapes=[center],
        compiler_params=params(),
        name="distances",
    )(sketch, first, second, before)


def nearest_kernel(sketch_size, each, parts, out):
    total = parts[0].astype(F32)
    for i in range(1, parts.shape[0]):
        total = total + parts[i].astype(F32)
    total = total / sketch_size
    half, rows = out.shape[0] // 2, out.shape[1]
    core = lax.axis_index("ex") % 2
    near = [jnp.min(total[r * each : (r + 1) * each, :], axis=0, keepdims=True) for r in range(half)]
    running = None
    for r in range(2 * half):
        own, other = near[r % half][:, :rows], near[r % half][:, rows:]
        row = jnp.where(core == r // half, own, other)
        running = row if running is None else jnp.minimum(running, row)
        out[r : r + 1, :] = running


def nearest(parts, sketch_size, rounds):
    vmem = pl.BlockSpec(memory_space=pltpu.VMEM)
    each = 2 * parts.shape[1] // rounds
    return pl.pallas_call(
        functools.partial(nearest_kernel, sketch_size, each),
        in_specs=[vmem],
        out_specs=vmem,
        out_shape=jax.ShapeDtypeStruct((rounds, parts.shape[2] // 2), F32),
        compiler_params=params(),
        name="nearest",
    )(parts)


def swap(x, axis, size, step):
    return lax.ppermute(x, axis, [(i, i ^ step) for i in range(size)])


def per_device(feat, ex, grads, first_factor, second_factor, picks):
    rows = grads.shape[0]
    local = first_factor.shape[0]
    groups, _, width = second_factor.shape
    near = feat // 2
    factor = jnp.swapaxes(first_factor, 1, 2)
    count = local // 2 if local % 64 == 0 else local
    start, half = local - count, count // 2
    pieces, plan = [], []
    if start:
        (inner,) = first_products(grads, factor, feat, False, 0, start)
        pieces.append([lax.all_to_all(inner, "feat", split_axis=0, concat_axis=0, tiled=True)])
        plan.append([(False, d, 0, start // 2) for d in range(feat)])
    split = first_products(grads, factor, feat, True, start, count)
    far = [swap(x, "feat", feat, near + i) for i, x in enumerate(split[near:])]
    close = [x if d == 0 else swap(x, "feat", feat, d) for d, x in enumerate(split[:near])]
    pieces += [close, far]
    plan += [[(True, d, start, half) for d in places] for places in (range(near), range(near, feat))]

    factors = turned(second_factor, local, plan)
    early = early_products(factors[:-1], pieces[:-1], rows)
    sketch, mine, other = late_products(picks, early, factors[-1:], pieces[-1:])

    chip = mine + swap(other, "ex", ex, 1)
    across = [chip]
    step = 2
    while step < ex:
        across = across + [swap(x, "ex", ex, step) for x in across]
        step *= 2
    across = [across[0], sum(across[1:])]
    kept, part = distances(sketch, *across)
    part = distances(sketch, *[swap(x, "ex", ex, 1) for x in across], before=part)
    spread = jnp.broadcast_to(part[None], (feat,) + part.shape)
    gathered = lax.all_to_all(spread, "feat", split_axis=0, concat_axis=0, tiled=True)
    coverage = nearest(gathered, feat * groups * width, picks.shape[0])
    return (kept, coverage)


def solution(mesh):
    feat, ex = mesh.shape["feat"], mesh.shape["ex"]
    in_specs = (P("ex", "feat"), P("feat", None, None), P("feat", None, None), P())
    out_specs = (P("ex", "feat"), P(None, "ex"))
    return jax.shard_map(
        functools.partial(per_device, feat, ex),
        mesh=mesh,
        in_specs=in_specs,
        out_specs=out_specs,
        check_vma=False,
    )
```

```python
import functools

import jax
import jax.numpy as jnp
from jax import lax
from jax.experimental import pallas as pl
from jax.experimental.pallas import tpu as pltpu
from jax.sharding import PartitionSpec as P

F32 = jnp.float32
BF16 = jnp.bfloat16
MIB = 1024 * 1024
UNROLL = 4
NT = (((1,), (1,)), ((), ()))
NN = (((1,), (0,)), ((), ()))


def params(mib=8):
    return pltpu.CompilerParams(vmem_limit_bytes=mib * MIB)


def first_kernel(feat, start, half, step, flush, *refs):
    grads, factor, *outs, g_buf, w_buf, acc, sems = refs
    _, groups, size = factor.shape
    kept = groups // feat
    steps = half // step
    split = len(outs) > 1
    me = lax.axis_index("feat") if split else 0

    def copies(i):
        for h in range(2):
            block = start + h * half + i * step
            yield pltpu.make_async_copy(
                grads.at[:, pl.ds(block * size, step * size)], g_buf.at[h, i], sems.at[h, i, 0]
            )
            yield pltpu.make_async_copy(factor.at[pl.ds(block, step)], w_buf.at[h, i], sems.at[h, i, 1])

    for i in range(steps):
        for copy in copies(i):
            copy.start()
    for i in range(steps):
        for copy in copies(i):
            copy.wait()
        for t in range(step):
            cols = slice(t * size, (t + 1) * size)
            low = lax.dot_general(w_buf[0, i, t], g_buf[0, i, :, cols], NT, preferred_element_type=F32)
            high = lax.dot_general(w_buf[1, i, t], g_buf[1, i, :, cols], NT, preferred_element_type=F32)
            acc[pl.ds(i * step + t, groups, stride=half), :] = jnp.concatenate([low, high], axis=1)
        if (i + 1) * step % flush == 0:
            done = (i + 1) * step - flush
            for d in range(feat):
                first = (me ^ d) * (kept * half)
                for q in range(kept):
                    at = pl.multiple_of(first + q * half + done, 8)
                    rows = acc[pl.ds(at, flush), :].astype(BF16)
                    if split:
                        outs[d][q, done : done + flush, :] = rows
                    else:
                        outs[0][d * kept + q, done : done + flush, :] = rows


def first_products(grads, factor, feat, split, start, count):
    rows = grads.shape[0]
    _, groups, size = factor.shape
    kept = groups // feat
    half = count // 2
    step, flush = min(4, half), min(16, half)
    steps = half // step
    lanes = 2 * rows
    if split:
        out_shape = [jax.ShapeDtypeStruct((kept, half, lanes), BF16)] * feat
    else:
        out_shape = [jax.ShapeDtypeStruct((groups, half, lanes), BF16)]
    vmem = pl.BlockSpec(memory_space=pltpu.VMEM)
    hbm = pl.BlockSpec(memory_space=pl.ANY)
    return pl.pallas_call(
        functools.partial(first_kernel, feat, start, half, step, flush),
        in_specs=[hbm, hbm],
        out_specs=[vmem] * len(out_shape),
        out_shape=out_shape,
        scratch_shapes=[
            pltpu.VMEM((2, steps, rows, step * size), BF16),
            pltpu.VMEM((2, steps, step, groups, size), BF16),
            pltpu.VMEM((groups * half, lanes), F32),
            pltpu.SemaphoreType.DMA((2, steps, 2)),
        ],
        compiler_params=params(48),
        cost_estimate=pl.CostEstimate(
            flops=2 * count * rows * groups * size,
            bytes_accessed=2 * count * size * (rows + groups),
            transcendentals=0,
        ),
        name="first_products",
    )(grads, factor)


def turn_kernel(plan, local, second, *outs):
    me = lax.axis_index("feat")
    width = second.shape[2]
    for spans, out in zip(plan, outs):
        for k in range(second.shape[0]):
            for h in range(2):
                rows = []
                for relative, source, start, half in spans:
                    if relative:
                        at = pl.multiple_of((me ^ source) * local + start + h * half, 8)
                    else:
                        at = source * local + start + h * half
                    rows.append(second[k, pl.ds(at, half), :])
                out[k, h * width : (h + 1) * width, :] = jnp.concatenate(rows, axis=0).T


def turned(second, local, plan):
    groups, _, width = second.shape
    vmem = pl.BlockSpec(memory_space=pltpu.VMEM)
    return pl.pallas_call(
        functools.partial(turn_kernel, plan, local),
        in_specs=[vmem],
        out_specs=[vmem] * len(plan),
        out_shape=[
            jax.ShapeDtypeStruct((groups, 2 * width, sum(span[-1] for span in spans)), BF16) for spans in plan
        ],
        compiler_params=params(),
        name="turned_factor",
    )(second)


def products(k, factors, pieces, rows):
    total = None
    for a, own in zip(factors, pieces):
        groups = a.shape[0]
        right = jnp.concatenate([x[at + k] for x in own for at in range(0, x.shape[0], groups)], axis=0)
        part = lax.dot_general(a[k], right, NN, preferred_element_type=F32)
        total = part if total is None else total + part
    width = total.shape[0] // 2
    return (total[:width, :rows] + total[width:, rows:]).T


def split_refs(counts, refs):
    refs = list(refs)
    factors = [refs.pop(0) for _ in counts]
    pieces = [[refs.pop(0) for _ in range(n)] for n in counts]
    return factors, pieces, refs


def early_kernel(counts, *refs):
    factors, pieces, (out,) = split_refs(counts, refs)
    groups, both, _ = factors[0].shape
    width = both // 2
    for k in range(groups):
        out[:, k * width : (k + 1) * width] = products(k, factors, pieces, out.shape[0])


def early_products(factors, pieces, rows):
    groups, both, _ = factors[0].shape
    vmem = pl.BlockSpec(memory_space=pltpu.VMEM)
    counts = [len(own) for own in pieces]
    return pl.pallas_call(
        functools.partial(early_kernel, counts),
        in_specs=[vmem] * (len(counts) + sum(counts)),
        out_specs=vmem,
        out_shape=jax.ShapeDtypeStruct((rows, groups * both // 2), F32),
        compiler_params=params(),
        name="early_products",
    )(*factors, *[x for own in pieces for x in own])


def late_kernel(counts, picks, early, *refs):
    factors, pieces, (sketch, mine, other, held) = split_refs(counts, refs)
    groups, both, _ = factors[0].shape
    width, rows = both // 2, sketch.shape[0]
    slots = mine.shape[1]
    if groups < slots:
        held[...] = jnp.zeros_like(held)
    for k in range(groups):
        cols = slice(k * width, (k + 1) * width)
        mapped = early[:, cols] + products(k, factors, pieces, rows)
        sketch[:, cols] = mapped
        held[pl.ds(k, rows, stride=slots), :] = mapped
    rounds, each = picks.shape
    place = lax.axis_index("ex")
    base, core = place * rows, place % 2
    half = rounds // 2
    for r in range(half):
        for p in range(each):
            for out, side in ((mine, core), (other, 1 - core)):
                at = picks[side * half + r, p] - base
                held_here = (at >= 0) & (at < rows)
                start = pl.multiple_of(jnp.clip(at, 0, rows - 1) * slots, slots)
                out[r * each + p] = jnp.where(held_here, held[pl.ds(start, slots), :], 0.0)


def late_products(picks, early, factors, pieces):
    rows = early.shape[0]
    groups, both, _ = factors[0].shape
    width = both // 2
    slots = -(-groups // 8) * 8
    smem = pl.BlockSpec(memory_space=pltpu.SMEM)
    vmem = pl.BlockSpec(memory_space=pltpu.VMEM)
    counts = [len(own) for own in pieces]
    fetched = jax.ShapeDtypeStruct((picks.size // 2, slots, width), F32)
    return pl.pallas_call(
        functools.partial(late_kernel, counts),
        in_specs=[smem] + [vmem] * (1 + len(counts) + sum(counts)),
        out_specs=[vmem] * 3,
        out_shape=[jax.ShapeDtypeStruct(early.shape, F32), fetched, fetched],
        scratch_shapes=[pltpu.VMEM((rows * slots, width), F32)],
        compiler_params=params(),
        name="late_products",
    )(picks, early, *factors, *[x for own in pieces for x in own])


def listed(picks, chosen, side, own, rows):
    rounds, each = picks.shape
    count = rounds * each // 2
    pair = lax.axis_index("ex") // 2

    def one(i, n):
        at = side * count + i
        here = picks[at // each, at % each] // (2 * rows) == pair
        chosen[n] = i
        return n + (here if own else jnp.logical_not(here)).astype(jnp.int32)

    n = lax.fori_loop(0, count, one, 0)
    last = chosen[jnp.maximum(n - 1, 0)]
    for extra in range(UNROLL - 1):
        chosen[n + extra] = last
    return (n + UNROLL - 1) // UNROLL


def add_distances(sums, sketch, center, chosen, groups, first_lane):
    rows, dims = sketch.shape
    width = center.shape[2]
    lane = lax.broadcasted_iota(jnp.int32, (8, 128), 1)

    def some(i, sums):
        sums = list(sums)
        places = [chosen[i * UNROLL + u] for u in range(UNROLL)]
        for g in range(rows // 8):
            block = [sketch[g * 8 : (g + 1) * 8, t * width : (t + 1) * width] for t in range(dims // width)]
            for p in places:
                acc = None
                for t, own in enumerate(block):
                    diff = own - center[p, t : t + 1, :]
                    acc = diff * diff if acc is None else acc + diff * diff
                sums[g] = jnp.where(lane == p + first_lane, jnp.sum(acc, axis=1, keepdims=True), sums[g])
        return tuple(sums)

    return lax.fori_loop(0, groups, some, tuple(sums))


def spread_sums(sums, rows):
    return [sums[g * 8 : (g + 1) * 8, :] for g in range(rows // 8)]


def held_kernel(picks, sketch, mine, other, kept, out, chosen, sem):
    copy = pltpu.make_async_copy(sketch, kept, sem)
    copy.start()
    rows = sketch.shape[0]
    core = lax.axis_index("ex") % 2
    sums = [jnp.zeros((8, 128), F32) for _ in range(rows // 8)]
    for side, center in enumerate((mine, other)):
        groups = listed(picks, chosen, core if side == 0 else 1 - core, True, rows)
        sums = add_distances(sums, sketch, center, chosen, groups, side * center.shape[0])
    for g, own in enumerate(sums):
        out[g * 8 : (g + 1) * 8, :] = own
    copy.wait()


def far_kernel(side, picks, sketch, center, before, out, chosen):
    rows, count = sketch.shape[0], center.shape[0]
    core = lax.axis_index("ex") % 2
    groups = listed(picks, chosen, core if side == 0 else 1 - core, False, rows)
    sums = add_distances(spread_sums(before, rows), sketch, center, chosen, groups, side * count)
    if side == 0:
        for g, own in enumerate(sums):
            out[g * 8 : (g + 1) * 8, :] = own
    else:
        by_pick = jnp.concatenate(sums, axis=0).T
        by_pick = jnp.concatenate([by_pick[:count], by_pick[count : 2 * count]], axis=1)
        out[...] = by_pick.astype(out.dtype)


def held_distances(picks, sketch, mine, other):
    vmem = pl.BlockSpec(memory_space=pltpu.VMEM)
    return pl.pallas_call(
        held_kernel,
        in_specs=[pl.BlockSpec(memory_space=pltpu.SMEM)] + [vmem] * 3,
        out_specs=[pl.BlockSpec(memory_space=pl.ANY), vmem],
        out_shape=[
            jax.ShapeDtypeStruct(sketch.shape, F32),
            jax.ShapeDtypeStruct((sketch.shape[0], 128), F32),
        ],
        scratch_shapes=[pltpu.SMEM((mine.shape[0] + UNROLL,), jnp.int32), pltpu.SemaphoreType.DMA],
        compiler_params=params(),
        name="held_distances",
    )(picks, sketch, mine, other)


def far_distances(side, picks, sketch, center, before):
    vmem = pl.BlockSpec(memory_space=pltpu.VMEM)
    count, rows = center.shape[0], sketch.shape[0]
    if side == 0:
        out = jax.ShapeDtypeStruct((rows, 128), F32)
    else:
        out = jax.ShapeDtypeStruct((count, 2 * rows), BF16)
    return pl.pallas_call(
        functools.partial(far_kernel, side),
        in_specs=[pl.BlockSpec(memory_space=pltpu.SMEM)] + [vmem] * 3,
        out_specs=vmem,
        out_shape=out,
        scratch_shapes=[pltpu.SMEM((count + UNROLL,), jnp.int32)],
        compiler_params=params(),
        name="far_distances",
    )(picks, sketch, center, before)


def nearest_kernel(sketch_size, each, parts, out):
    total = parts[0].astype(F32)
    for i in range(1, parts.shape[0]):
        total = total + parts[i].astype(F32)
    total = total / sketch_size
    half, rows = out.shape[0] // 2, out.shape[1]
    core = lax.axis_index("ex") % 2
    near = [jnp.min(total[r * each : (r + 1) * each, :], axis=0, keepdims=True) for r in range(half)]
    running = None
    for r in range(2 * half):
        own, other = near[r % half][:, :rows], near[r % half][:, rows:]
        row = jnp.where(core == r // half, own, other)
        running = row if running is None else jnp.minimum(running, row)
        out[r : r + 1, :] = running


def nearest(parts, sketch_size, rounds):
    vmem = pl.BlockSpec(memory_space=pltpu.VMEM)
    each = 2 * parts.shape[1] // rounds
    return pl.pallas_call(
        functools.partial(nearest_kernel, sketch_size, each),
        in_specs=[vmem],
        out_specs=vmem,
        out_shape=jax.ShapeDtypeStruct((rounds, parts.shape[2] // 2), F32),
        compiler_params=params(),
        name="nearest",
    )(parts)


def swap(x, axis, size, step):
    return lax.ppermute(x, axis, [(i, i ^ step) for i in range(size)])


def per_device(feat, ex, grads, first_factor, second_factor, picks):
    rows = grads.shape[0]
    local = first_factor.shape[0]
    groups, _, width = second_factor.shape
    near = feat // 2
    factor = jnp.swapaxes(first_factor, 1, 2)
    count = local // 2 if local % 64 == 0 else local
    start, half = local - count, count // 2
    pieces, plan = [], []
    if start:
        (inner,) = first_products(grads, factor, feat, False, 0, start)
        pieces.append([lax.all_to_all(inner, "feat", split_axis=0, concat_axis=0, tiled=True)])
        plan.append([(False, d, 0, start // 2) for d in range(feat)])
    split = first_products(grads, factor, feat, True, start, count)
    far = [swap(x, "feat", feat, near + i) for i, x in enumerate(split[near:])]
    close = [x if d == 0 else swap(x, "feat", feat, d) for d, x in enumerate(split[:near])]
    pieces += [close, far]
    plan += [[(True, d, start, half) for d in places] for places in (range(near), range(near, feat))]

    factors = turned(second_factor, local, plan)
    early = early_products(factors[:-1], pieces[:-1], rows)
    sketch, mine, other = late_products(picks, early, factors[-1:], pieces[-1:])

    held = mine + swap(other, "ex", ex, 1)
    across, step = [held], 2
    while step < ex:
        across = across + [swap(x, "ex", ex, step) for x in across]
        step *= 2
    away = sum(across[2:], across[1])
    kept, part = held_distances(picks, sketch, held, swap(held, "ex", ex, 1))
    part = far_distances(0, picks, sketch, away, part)
    part = far_distances(1, picks, sketch, swap(away, "ex", ex, 1), part)
    spread = jnp.broadcast_to(part[None], (feat,) + part.shape)
    gathered = lax.all_to_all(spread, "feat", split_axis=0, concat_axis=0, tiled=True)
    coverage = nearest(gathered, feat * groups * width, picks.shape[0])
    return (kept, coverage)


def solution(mesh):
    feat, ex = mesh.shape["feat"], mesh.shape["ex"]
    in_specs = (P("ex", "feat"), P("feat", None, None), P("feat", None, None), P())
    out_specs = (P("ex", "feat"), P(None, "ex"))
    return jax.shard_map(
        functools.partial(per_device, feat, ex),
        mesh=mesh,
        in_specs=in_specs,
        out_specs=out_specs,
        check_vma=False,
    )
```

```python
import functools

import jax
import jax.numpy as jnp
from jax import lax
from jax.experimental import pallas as pl
from jax.experimental.pallas import tpu as pltpu
from jax.sharding import PartitionSpec as P

F32 = jnp.float32
BF16 = jnp.bfloat16
MIB = 1024 * 1024
NT = (((1,), (1,)), ((), ()))
NN = (((1,), (0,)), ((), ()))


def params(mib=8):
    return pltpu.CompilerParams(vmem_limit_bytes=mib * MIB)


def first_kernel(feat, start, half, step, flush, *refs):
    grads, factor, *outs, g_buf, w_buf, acc, sems = refs
    _, groups, size = factor.shape
    kept = groups // feat
    steps = half // step
    split = len(outs) > 1
    me = lax.axis_index("feat") if split else 0

    def copies(i):
        for h in range(2):
            block = start + h * half + i * step
            yield pltpu.make_async_copy(
                grads.at[:, pl.ds(block * size, step * size)], g_buf.at[h, i], sems.at[h, i, 0]
            )
            yield pltpu.make_async_copy(factor.at[pl.ds(block, step)], w_buf.at[h, i], sems.at[h, i, 1])

    for i in range(steps):
        for copy in copies(i):
            copy.start()
    for i in range(steps):
        for copy in copies(i):
            copy.wait()
        for t in range(step):
            cols = slice(t * size, (t + 1) * size)
            low = lax.dot_general(w_buf[0, i, t], g_buf[0, i, :, cols], NT, preferred_element_type=F32)
            high = lax.dot_general(w_buf[1, i, t], g_buf[1, i, :, cols], NT, preferred_element_type=F32)
            acc[pl.ds(i * step + t, groups, stride=half), :] = jnp.concatenate([low, high], axis=1)
        if (i + 1) * step % flush == 0:
            done = (i + 1) * step - flush
            for d in range(feat):
                first = (me ^ d) * (kept * half)
                for q in range(kept):
                    at = pl.multiple_of(first + q * half + done, 8)
                    rows = acc[pl.ds(at, flush), :].astype(BF16)
                    if split:
                        outs[d][q, done : done + flush, :] = rows
                    else:
                        outs[0][d * kept + q, done : done + flush, :] = rows


def first_products(grads, factor, feat, split, start, count):
    rows = grads.shape[0]
    _, groups, size = factor.shape
    kept = groups // feat
    half = count // 2
    step, flush = min(4, half), min(16, half)
    steps = half // step
    lanes = 2 * rows
    if split:
        out_shape = [jax.ShapeDtypeStruct((kept, half, lanes), BF16)] * feat
    else:
        out_shape = [jax.ShapeDtypeStruct((groups, half, lanes), BF16)]
    vmem = pl.BlockSpec(memory_space=pltpu.VMEM)
    hbm = pl.BlockSpec(memory_space=pl.ANY)
    return pl.pallas_call(
        functools.partial(first_kernel, feat, start, half, step, flush),
        in_specs=[hbm, hbm],
        out_specs=[vmem] * len(out_shape),
        out_shape=out_shape,
        scratch_shapes=[
            pltpu.VMEM((2, steps, rows, step * size), BF16),
            pltpu.VMEM((2, steps, step, groups, size), BF16),
            pltpu.VMEM((groups * half, lanes), F32),
            pltpu.SemaphoreType.DMA((2, steps, 2)),
        ],
        compiler_params=params(48),
        cost_estimate=pl.CostEstimate(
            flops=2 * count * rows * groups * size,
            bytes_accessed=2 * count * size * (rows + groups),
            transcendentals=0,
        ),
        name="first_products",
    )(grads, factor)


def turn_kernel(plan, local, second, *outs):
    me = lax.axis_index("feat")
    width = second.shape[2]
    for spans, out in zip(plan, outs):
        for k in range(second.shape[0]):
            for h in range(2):
                rows = []
                for relative, source, start, half in spans:
                    if relative:
                        at = pl.multiple_of((me ^ source) * local + start + h * half, 8)
                    else:
                        at = source * local + start + h * half
                    rows.append(second[k, pl.ds(at, half), :])
                out[k, h * width : (h + 1) * width, :] = jnp.concatenate(rows, axis=0).T


def turned(second, local, plan):
    groups, _, width = second.shape
    vmem = pl.BlockSpec(memory_space=pltpu.VMEM)
    return pl.pallas_call(
        functools.partial(turn_kernel, plan, local),
        in_specs=[vmem],
        out_specs=[vmem] * len(plan),
        out_shape=[
            jax.ShapeDtypeStruct((groups, 2 * width, sum(span[-1] for span in spans)), BF16) for spans in plan
        ],
        compiler_params=params(),
        name="turned_factor",
    )(second)


def products(k, factors, pieces, rows):
    total = None
    for a, own in zip(factors, pieces):
        groups = a.shape[0]
        right = jnp.concatenate([x[at + k] for x in own for at in range(0, x.shape[0], groups)], axis=0)
        part = lax.dot_general(a[k], right, NN, preferred_element_type=F32)
        total = part if total is None else total + part
    width = total.shape[0] // 2
    return (total[:width, :rows] + total[width:, rows:]).T


def split_refs(counts, refs):
    refs = list(refs)
    factors = [refs.pop(0) for _ in counts]
    pieces = [[refs.pop(0) for _ in range(n)] for n in counts]
    return factors, pieces, refs


def early_kernel(counts, *refs):
    factors, pieces, (out,) = split_refs(counts, refs)
    groups, both, _ = factors[0].shape
    width = both // 2
    for k in range(groups):
        out[:, k * width : (k + 1) * width] = products(k, factors, pieces, out.shape[0])


def early_products(factors, pieces, rows):
    groups, both, _ = factors[0].shape
    vmem = pl.BlockSpec(memory_space=pltpu.VMEM)
    counts = [len(own) for own in pieces]
    return pl.pallas_call(
        functools.partial(early_kernel, counts),
        in_specs=[vmem] * (len(counts) + sum(counts)),
        out_specs=vmem,
        out_shape=jax.ShapeDtypeStruct((rows, groups * both // 2), F32),
        compiler_params=params(),
        name="early_products",
    )(*factors, *[x for own in pieces for x in own])


def late_kernel(counts, picks, early, *refs):
    factors, pieces, (sketch, mine, other, held) = split_refs(counts, refs)
    groups, both, _ = factors[0].shape
    width, rows = both // 2, sketch.shape[0]
    slots = mine.shape[1]
    if groups < slots:
        held[...] = jnp.zeros_like(held)
    for k in range(groups):
        cols = slice(k * width, (k + 1) * width)
        mapped = early[:, cols] + products(k, factors, pieces, rows)
        sketch[:, cols] = mapped
        held[pl.ds(k, rows, stride=slots), :] = mapped
    rounds, each = picks.shape
    place = lax.axis_index("ex")
    base, core = place * rows, place % 2
    half = rounds // 2
    for r in range(half):
        for p in range(each):
            for out, side in ((mine, core), (other, 1 - core)):
                at = picks[side * half + r, p] - base
                held_here = (at >= 0) & (at < rows)
                start = pl.multiple_of(jnp.clip(at, 0, rows - 1) * slots, slots)
                out[r * each + p] = jnp.where(held_here, held[pl.ds(start, slots), :], 0.0)


def late_products(picks, early, factors, pieces):
    rows = early.shape[0]
    groups, both, _ = factors[0].shape
    width = both // 2
    slots = -(-groups // 8) * 8
    smem = pl.BlockSpec(memory_space=pltpu.SMEM)
    vmem = pl.BlockSpec(memory_space=pltpu.VMEM)
    counts = [len(own) for own in pieces]
    fetched = jax.ShapeDtypeStruct((picks.size // 2, slots, width), F32)
    return pl.pallas_call(
        functools.partial(late_kernel, counts),
        in_specs=[smem] + [vmem] * (1 + len(counts) + sum(counts)),
        out_specs=[vmem] * 3,
        out_shape=[jax.ShapeDtypeStruct(early.shape, F32), fetched, fetched],
        scratch_shapes=[pltpu.VMEM((rows * slots, width), F32)],
        compiler_params=params(),
        name="late_products",
    )(picks, early, *factors, *[x for own in pieces for x in own])


def distance_kernel(unroll, sketch, first, second, *refs):
    if len(refs) == 4:
        kept, out, center, sem = refs
        before = None
        copy = pltpu.make_async_copy(sketch, kept, sem)
        copy.start()
    else:
        before, out, center = refs
        copy = None
    rows, dims = sketch.shape
    count, _, width = center.shape
    center[...] = first[...] + second[...]
    lane = lax.broadcasted_iota(jnp.int32, (8, 128), 1)
    sums = [jnp.zeros((8, 128), F32)] * (rows // 8)
    for p in range(0, count, unroll):
        for g in range(rows // 8):
            block = [sketch[g * 8 : (g + 1) * 8, t * width : (t + 1) * width] for t in range(dims // width)]
            for u in range(unroll):
                acc = None
                for t, own in enumerate(block):
                    diff = own - center[p + u, t : t + 1, :]
                    acc = diff * diff if acc is None else acc + diff * diff
                sums[g] = jnp.where(lane == p + u, jnp.sum(acc, axis=1, keepdims=True), sums[g])
    by_pick = jnp.concatenate(sums, axis=0).T[:count]
    if before is not None:
        by_pick = jnp.concatenate([before[...], by_pick], axis=1)
    out[...] = by_pick.astype(out.dtype)
    if copy is not None:
        copy.wait()


def distances(sketch, first, second, before=None):
    vmem = pl.BlockSpec(memory_space=pltpu.VMEM)
    hbm = pl.BlockSpec(memory_space=pl.ANY)
    count, rows = first.shape[0], sketch.shape[0]
    center = pltpu.VMEM(first.shape, F32)
    if before is None:
        return pl.pallas_call(
            functools.partial(distance_kernel, 4),
            in_specs=[vmem] * 3,
            out_specs=[hbm, vmem],
            out_shape=[jax.ShapeDtypeStruct(sketch.shape, F32), jax.ShapeDtypeStruct((count, rows), F32)],
            scratch_shapes=[center, pltpu.SemaphoreType.DMA],
            compiler_params=params(),
            name="distances",
        )(sketch, first, second)
    return pl.pallas_call(
        functools.partial(distance_kernel, 4),
        in_specs=[vmem] * 4,
        out_specs=vmem,
        out_shape=jax.ShapeDtypeStruct((count, 2 * rows), BF16),
        scratch_shapes=[center],
        compiler_params=params(),
        name="distances",
    )(sketch, first, second, before)


def nearest_kernel(sketch_size, each, parts, out):
    total = parts[0].astype(F32)
    for i in range(1, parts.shape[0]):
        total = total + parts[i].astype(F32)
    total = total / sketch_size
    half, rows = out.shape[0] // 2, out.shape[1]
    core = lax.axis_index("ex") % 2
    near = [jnp.min(total[r * each : (r + 1) * each, :], axis=0, keepdims=True) for r in range(half)]
    running = None
    for r in range(2 * half):
        own, other = near[r % half][:, :rows], near[r % half][:, rows:]
        row = jnp.where(core == r // half, own, other)
        running = row if running is None else jnp.minimum(running, row)
        out[r : r + 1, :] = running


def nearest(parts, sketch_size, rounds):
    vmem = pl.BlockSpec(memory_space=pltpu.VMEM)
    each = 2 * parts.shape[1] // rounds
    return pl.pallas_call(
        functools.partial(nearest_kernel, sketch_size, each),
        in_specs=[vmem],
        out_specs=vmem,
        out_shape=jax.ShapeDtypeStruct((rounds, parts.shape[2] // 2), F32),
        compiler_params=params(),
        name="nearest",
    )(parts)


def swap(x, axis, size, step):
    return lax.ppermute(x, axis, [(i, i ^ step) for i in range(size)])


def per_device(feat, ex, grads, first_factor, second_factor, picks):
    rows = grads.shape[0]
    local = first_factor.shape[0]
    groups, _, width = second_factor.shape
    near = feat // 2
    factor = jnp.swapaxes(first_factor, 1, 2)
    count = local // 2 if local % 64 == 0 else local
    start, half = local - count, count // 2
    pieces, plan = [], []
    if start:
        (inner,) = first_products(grads, factor, feat, False, 0, start)
        pieces.append([lax.all_to_all(inner, "feat", split_axis=0, concat_axis=0, tiled=True)])
        plan.append([(False, d, 0, start // 2) for d in range(feat)])
    split = first_products(grads, factor, feat, True, start, count)
    far = [swap(x, "feat", feat, near + i) for i, x in enumerate(split[near:])]
    close = [x if d == 0 else swap(x, "feat", feat, d) for d, x in enumerate(split[:near])]
    pieces += [close, far]
    plan += [[(True, d, start, half) for d in places] for places in (range(near), range(near, feat))]

    factors = turned(second_factor, local, plan)
    early = early_products(factors[:-1], pieces[:-1], rows)
    sketch, mine, other = late_products(picks, early, factors[-1:], pieces[-1:])

    chip = mine + swap(other, "ex", ex, 1)
    across = [chip]
    step = 2
    while step < ex:
        across = across + [swap(x, "ex", ex, step) for x in across]
        step *= 2
    across = [across[0], sum(across[1:])]
    kept, part = distances(sketch, *across)
    part = distances(sketch, *[swap(x, "ex", ex, 1) for x in across], before=part)
    spread = jnp.broadcast_to(part[None], (feat,) + part.shape)
    gathered = lax.all_to_all(spread, "feat", split_axis=0, concat_axis=0, tiled=True)
    coverage = nearest(gathered, feat * groups * width, picks.shape[0])
    return (kept, coverage)


def solution(mesh):
    feat, ex = mesh.shape["feat"], mesh.shape["ex"]
    in_specs = (P("ex", "feat"), P("feat", None, None), P("feat", None, None), P())
    out_specs = (P("ex", "feat"), P(None, "ex"))
    return jax.shard_map(
        functools.partial(per_device, feat, ex),
        mesh=mesh,
        in_specs=in_specs,
        out_specs=out_specs,
        check_vma=False,
    )
```

```python
import functools

import jax
import jax.numpy as jnp
from jax import lax
from jax.experimental import pallas as pl
from jax.experimental.pallas import tpu as pltpu
from jax.sharding import PartitionSpec as P

F32 = jnp.float32
BF16 = jnp.bfloat16
MIB = 1024 * 1024
NT = (((1,), (1,)), ((), ()))
NN = (((1,), (0,)), ((), ()))


def params(mib=8):
    return pltpu.CompilerParams(vmem_limit_bytes=mib * MIB)


def first_kernel(feat, start, half, step, flush, *refs):
    grads, factor, *outs, g_buf, w_buf, acc, sems = refs
    _, groups, size = factor.shape
    kept = groups // feat
    steps = half // step
    split = len(outs) > 1
    me = lax.axis_index("feat") if split else 0

    def copies(i):
        for h in range(2):
            block = start + h * half + i * step
            yield pltpu.make_async_copy(
                grads.at[:, pl.ds(block * size, step * size)], g_buf.at[h, i], sems.at[h, i, 0]
            )
            yield pltpu.make_async_copy(factor.at[pl.ds(block, step)], w_buf.at[h, i], sems.at[h, i, 1])

    for i in range(steps):
        for copy in copies(i):
            copy.start()
    for i in range(steps):
        for copy in copies(i):
            copy.wait()
        for t in range(step):
            cols = slice(t * size, (t + 1) * size)
            low = lax.dot_general(w_buf[0, i, t], g_buf[0, i, :, cols], NT, preferred_element_type=F32)
            high = lax.dot_general(w_buf[1, i, t], g_buf[1, i, :, cols], NT, preferred_element_type=F32)
            acc[pl.ds(i * step + t, groups, stride=half), :] = jnp.concatenate([low, high], axis=1)
        if (i + 1) * step % flush == 0:
            done = (i + 1) * step - flush
            for d in range(feat):
                first = (me ^ d) * (kept * half)
                for q in range(kept):
                    at = pl.multiple_of(first + q * half + done, 8)
                    rows = acc[pl.ds(at, flush), :].astype(BF16)
                    if split:
                        outs[d][q, done : done + flush, :] = rows
                    else:
                        outs[0][d * kept + q, done : done + flush, :] = rows


def first_products(grads, factor, feat, split, start, count):
    rows = grads.shape[0]
    _, groups, size = factor.shape
    kept = groups // feat
    half = count // 2
    step, flush = min(4, half), min(16, half)
    steps = half // step
    lanes = 2 * rows
    if split:
        out_shape = [jax.ShapeDtypeStruct((kept, half, lanes), BF16)] * feat
    else:
        out_shape = [jax.ShapeDtypeStruct((groups, half, lanes), BF16)]
    vmem = pl.BlockSpec(memory_space=pltpu.VMEM)
    hbm = pl.BlockSpec(memory_space=pl.ANY)
    return pl.pallas_call(
        functools.partial(first_kernel, feat, start, half, step, flush),
        in_specs=[hbm, hbm],
        out_specs=[vmem] * len(out_shape),
        out_shape=out_shape,
        scratch_shapes=[
            pltpu.VMEM((2, steps, rows, step * size), BF16),
            pltpu.VMEM((2, steps, step, groups, size), BF16),
            pltpu.VMEM((groups * half, lanes), F32),
            pltpu.SemaphoreType.DMA((2, steps, 2)),
        ],
        compiler_params=params(48),
        cost_estimate=pl.CostEstimate(
            flops=2 * count * rows * groups * size,
            bytes_accessed=2 * count * size * (rows + groups),
            transcendentals=0,
        ),
        name="first_products",
    )(grads, factor)


def turn_kernel(plan, local, second, *outs):
    me = lax.axis_index("feat")
    width = second.shape[2]
    for spans, out in zip(plan, outs):
        for k in range(second.shape[0]):
            for h in range(2):
                rows = []
                for relative, source, start, half in spans:
                    if relative:
                        at = pl.multiple_of((me ^ source) * local + start + h * half, 8)
                    else:
                        at = source * local + start + h * half
                    rows.append(second[k, pl.ds(at, half), :])
                depth = out.shape[2] // 2
                out[k, :, h * depth : (h + 1) * depth] = jnp.concatenate(rows, axis=0).T


def turned(second, local, plan):
    groups, _, width = second.shape
    vmem = pl.BlockSpec(memory_space=pltpu.VMEM)
    return pl.pallas_call(
        functools.partial(turn_kernel, plan, local),
        in_specs=[vmem],
        out_specs=[vmem] * len(plan),
        out_shape=[
            jax.ShapeDtypeStruct((groups, width, 2 * sum(span[-1] for span in spans)), BF16) for spans in plan
        ],
        compiler_params=params(),
        name="turned_factor",
    )(second)


def products(k, factors, pieces, rows):
    total = None
    for a, own in zip(factors, pieces):
        groups = a.shape[0]
        right = jnp.concatenate([x[at + k] for x in own for at in range(0, x.shape[0], groups)], axis=0)
        right = jnp.concatenate([right[:, :rows], right[:, rows:]], axis=0)
        part = lax.dot_general(a[k], right, NN, preferred_element_type=F32)
        total = part if total is None else total + part
    return total.T


def split_refs(counts, refs):
    refs = list(refs)
    factors = [refs.pop(0) for _ in counts]
    pieces = [[refs.pop(0) for _ in range(n)] for n in counts]
    return factors, pieces, refs


def early_kernel(counts, *refs):
    factors, pieces, (out,) = split_refs(counts, refs)
    groups, width, _ = factors[0].shape
    for k in range(groups):
        out[:, k * width : (k + 1) * width] = products(k, factors, pieces, out.shape[0])


def early_products(factors, pieces, rows):
    groups, width, _ = factors[0].shape
    vmem = pl.BlockSpec(memory_space=pltpu.VMEM)
    counts = [len(own) for own in pieces]
    return pl.pallas_call(
        functools.partial(early_kernel, counts),
        in_specs=[vmem] * (len(counts) + sum(counts)),
        out_specs=vmem,
        out_shape=jax.ShapeDtypeStruct((rows, groups * width), F32),
        compiler_params=params(),
        name="early_products",
    )(*factors, *[x for own in pieces for x in own])


def late_kernel(counts, picks, early, *refs):
    factors, pieces, (sketch, mine, other, held) = split_refs(counts, refs)
    groups, width, _ = factors[0].shape
    rows = sketch.shape[0]
    slots = mine.shape[1]
    if groups < slots:
        held[...] = jnp.zeros_like(held)
    for k in range(groups):
        cols = slice(k * width, (k + 1) * width)
        mapped = early[:, cols] + products(k, factors, pieces, rows)
        sketch[:, cols] = mapped
        held[pl.ds(k, rows, stride=slots), :] = mapped
    rounds, each = picks.shape
    place = lax.axis_index("ex")
    base, core = place * rows, place % 2
    half = rounds // 2
    for r in range(half):
        for p in range(each):
            for out, side in ((mine, core), (other, 1 - core)):
                at = picks[side * half + r, p] - base
                held_here = (at >= 0) & (at < rows)
                start = pl.multiple_of(jnp.clip(at, 0, rows - 1) * slots, slots)
                out[r * each + p] = jnp.where(held_here, held[pl.ds(start, slots), :], 0.0)


def late_products(picks, early, factors, pieces):
    rows = early.shape[0]
    groups, width, _ = factors[0].shape
    slots = -(-groups // 8) * 8
    smem = pl.BlockSpec(memory_space=pltpu.SMEM)
    vmem = pl.BlockSpec(memory_space=pltpu.VMEM)
    counts = [len(own) for own in pieces]
    fetched = jax.ShapeDtypeStruct((picks.size // 2, slots, width), F32)
    return pl.pallas_call(
        functools.partial(late_kernel, counts),
        in_specs=[smem] + [vmem] * (1 + len(counts) + sum(counts)),
        out_specs=[vmem] * 3,
        out_shape=[jax.ShapeDtypeStruct(early.shape, F32), fetched, fetched],
        scratch_shapes=[pltpu.VMEM((rows * slots, width), F32)],
        compiler_params=params(),
        name="late_products",
    )(picks, early, *factors, *[x for own in pieces for x in own])


def distance_kernel(unroll, sketch, first, second, *refs):
    if len(refs) == 4:
        kept, out, center, sem = refs
        before = None
        copy = pltpu.make_async_copy(sketch, kept, sem)
        copy.start()
    else:
        before, out, center = refs
        copy = None
    rows, dims = sketch.shape
    count, _, width = center.shape
    center[...] = first[...] + second[...]
    lane = lax.broadcasted_iota(jnp.int32, (8, 128), 1)
    sums = [jnp.zeros((8, 128), F32)] * (rows // 8)
    for p in range(0, count, unroll):
        for g in range(rows // 8):
            block = [sketch[g * 8 : (g + 1) * 8, t * width : (t + 1) * width] for t in range(dims // width)]
            for u in range(unroll):
                acc = None
                for t, own in enumerate(block):
                    diff = own - center[p + u, t : t + 1, :]
                    acc = diff * diff if acc is None else acc + diff * diff
                sums[g] = jnp.where(lane == p + u, jnp.sum(acc, axis=1, keepdims=True), sums[g])
    by_pick = jnp.concatenate(sums, axis=0).T[:count]
    if before is not None:
        by_pick = jnp.concatenate([before[...], by_pick], axis=1)
    out[...] = by_pick.astype(out.dtype)
    if copy is not None:
        copy.wait()


def distances(sketch, first, second, before=None):
    vmem = pl.BlockSpec(memory_space=pltpu.VMEM)
    hbm = pl.BlockSpec(memory_space=pl.ANY)
    count, rows = first.shape[0], sketch.shape[0]
    center = pltpu.VMEM(first.shape, F32)
    if before is None:
        return pl.pallas_call(
            functools.partial(distance_kernel, 4),
            in_specs=[vmem] * 3,
            out_specs=[hbm, vmem],
            out_shape=[jax.ShapeDtypeStruct(sketch.shape, F32), jax.ShapeDtypeStruct((count, rows), F32)],
            scratch_shapes=[center, pltpu.SemaphoreType.DMA],
            compiler_params=params(),
            name="distances",
        )(sketch, first, second)
    return pl.pallas_call(
        functools.partial(distance_kernel, 4),
        in_specs=[vmem] * 4,
        out_specs=vmem,
        out_shape=jax.ShapeDtypeStruct((count, 2 * rows), BF16),
        scratch_shapes=[center],
        compiler_params=params(),
        name="distances",
    )(sketch, first, second, before)


def nearest_kernel(sketch_size, each, parts, out):
    total = parts[0].astype(F32)
    for i in range(1, parts.shape[0]):
        total = total + parts[i].astype(F32)
    total = total / sketch_size
    half, rows = out.shape[0] // 2, out.shape[1]
    core = lax.axis_index("ex") % 2
    near = [jnp.min(total[r * each : (r + 1) * each, :], axis=0, keepdims=True) for r in range(half)]
    running = None
    for r in range(2 * half):
        own, other = near[r % half][:, :rows], near[r % half][:, rows:]
        row = jnp.where(core == r // half, own, other)
        running = row if running is None else jnp.minimum(running, row)
        out[r : r + 1, :] = running


def nearest(parts, sketch_size, rounds):
    vmem = pl.BlockSpec(memory_space=pltpu.VMEM)
    each = 2 * parts.shape[1] // rounds
    return pl.pallas_call(
        functools.partial(nearest_kernel, sketch_size, each),
        in_specs=[vmem],
        out_specs=vmem,
        out_shape=jax.ShapeDtypeStruct((rounds, parts.shape[2] // 2), F32),
        compiler_params=params(),
        name="nearest",
    )(parts)


def swap(x, axis, size, step):
    return lax.ppermute(x, axis, [(i, i ^ step) for i in range(size)])


def per_device(feat, ex, grads, first_factor, second_factor, picks):
    rows = grads.shape[0]
    local = first_factor.shape[0]
    groups, _, width = second_factor.shape
    near = feat // 2
    factor = jnp.swapaxes(first_factor, 1, 2)
    count = local // 2 if local % 64 == 0 else local
    start, half = local - count, count // 2
    pieces, plan = [], []
    if start:
        (inner,) = first_products(grads, factor, feat, False, 0, start)
        pieces.append([lax.all_to_all(inner, "feat", split_axis=0, concat_axis=0, tiled=True)])
        plan.append([(False, d, 0, start // 2) for d in range(feat)])
    split = first_products(grads, factor, feat, True, start, count)
    far = [swap(x, "feat", feat, near + i) for i, x in enumerate(split[near:])]
    close = [x if d == 0 else swap(x, "feat", feat, d) for d, x in enumerate(split[:near])]
    pieces += [close, far]
    plan += [[(True, d, start, half) for d in places] for places in (range(near), range(near, feat))]

    factors = turned(second_factor, local, plan)
    early = early_products(factors[:-1], pieces[:-1], rows)
    sketch, mine, other = late_products(picks, early, factors[-1:], pieces[-1:])

    chip = mine + swap(other, "ex", ex, 1)
    across = [chip]
    step = 2
    while step < ex:
        across = across + [swap(x, "ex", ex, step) for x in across]
        step *= 2
    across = [across[0], sum(across[1:])]
    kept, part = distances(sketch, *across)
    part = distances(sketch, *[swap(x, "ex", ex, 1) for x in across], before=part)
    spread = jnp.broadcast_to(part[None], (feat,) + part.shape)
    gathered = lax.all_to_all(spread, "feat", split_axis=0, concat_axis=0, tiled=True)
    coverage = nearest(gathered, feat * groups * width, picks.shape[0])
    return (kept, coverage)


def solution(mesh):
    feat, ex = mesh.shape["feat"], mesh.shape["ex"]
    in_specs = (P("ex", "feat"), P("feat", None, None), P("feat", None, None), P())
    out_specs = (P("ex", "feat"), P(None, "ex"))
    return jax.shard_map(
        functools.partial(per_device, feat, ex),
        mesh=mesh,
        in_specs=in_specs,
        out_specs=out_specs,
        check_vma=False,
    )
```

```python
import functools

import jax
import jax.numpy as jnp
from jax import lax
from jax.experimental import pallas as pl
from jax.experimental.pallas import tpu as pltpu
from jax.sharding import PartitionSpec as P

F32 = jnp.float32
BF16 = jnp.bfloat16
MIB = 1024 * 1024
NT = (((1,), (1,)), ((), ()))
NN = (((1,), (0,)), ((), ()))


def params(mib=8):
    return pltpu.CompilerParams(vmem_limit_bytes=mib * MIB)


def first_kernel(feat, pair, start, half, step, flush, *refs):
    grads, factor, *outs, g_buf, w_buf, acc, sems = refs
    _, groups, size = factor.shape
    kept = groups // feat
    steps = half // step
    split = len(outs) > 1
    me = lax.axis_index("feat") if split else 0

    def copies(i):
        for h in range(2):
            block = start + h * half + i * step
            yield pltpu.make_async_copy(
                grads.at[:, pl.ds(block * size, step * size)], g_buf.at[h, i], sems.at[h, i, 0]
            )
            yield pltpu.make_async_copy(factor.at[pl.ds(block, step)], w_buf.at[h, i], sems.at[h, i, 1])

    for i in range(steps):
        for copy in copies(i):
            copy.start()
    for i in range(steps):
        for copy in copies(i):
            copy.wait()
        for t in range(step):
            cols = slice(t * size, (t + 1) * size)
            low = lax.dot_general(w_buf[0, i, t], g_buf[0, i, :, cols], NT, preferred_element_type=F32)
            high = lax.dot_general(w_buf[1, i, t], g_buf[1, i, :, cols], NT, preferred_element_type=F32)
            acc[pl.ds(i * step + t, groups, stride=half), :] = jnp.concatenate([low, high], axis=1)
        if (i + 1) * step % flush == 0:
            done = (i + 1) * step - flush
            for d in range(feat):
                first = (me ^ d) * (kept * half)
                for q in range(kept):
                    at = pl.multiple_of(first + q * half + done, 8)
                    rows = acc[pl.ds(at, flush), :].astype(BF16)
                    if split and pair and d in (2, 3):
                        outs[2][(d - 2) * kept + q, done : done + flush, :] = rows
                    elif split:
                        outs[d - 1 if pair and d > 3 else d][q, done : done + flush, :] = rows
                    else:
                        outs[0][d * kept + q, done : done + flush, :] = rows


def first_products(grads, factor, feat, pair, split, start, count):
    rows = grads.shape[0]
    _, groups, size = factor.shape
    kept = groups // feat
    half = count // 2
    step, flush = min(4, half), min(16, half)
    steps = half // step
    lanes = 2 * rows
    if split:
        out_shape = [jax.ShapeDtypeStruct((kept, half, lanes), BF16)] * feat
        if pair:
            out_shape[2:4] = [jax.ShapeDtypeStruct((2 * kept, half, lanes), BF16)]
    else:
        out_shape = [jax.ShapeDtypeStruct((groups, half, lanes), BF16)]
    vmem = pl.BlockSpec(memory_space=pltpu.VMEM)
    hbm = pl.BlockSpec(memory_space=pl.ANY)
    return pl.pallas_call(
        functools.partial(first_kernel, feat, pair, start, half, step, flush),
        in_specs=[hbm, hbm],
        out_specs=[vmem] * len(out_shape),
        out_shape=out_shape,
        scratch_shapes=[
            pltpu.VMEM((2, steps, rows, step * size), BF16),
            pltpu.VMEM((2, steps, step, groups, size), BF16),
            pltpu.VMEM((groups * half, lanes), F32),
            pltpu.SemaphoreType.DMA((2, steps, 2)),
        ],
        compiler_params=params(48),
        cost_estimate=pl.CostEstimate(
            flops=2 * count * rows * groups * size,
            bytes_accessed=2 * count * size * (rows + groups),
            transcendentals=0,
        ),
        name="first_products",
    )(grads, factor)


def pack_kernel(own, beside, across, near, message):
    kept = own.shape[0]
    near[:kept] = own[...]
    near[kept:] = across[:kept]
    message[:kept] = beside[...]
    message[kept:] = across[kept:]


def packed(own, beside, across):
    vmem = pl.BlockSpec(memory_space=pltpu.VMEM)
    return pl.pallas_call(
        pack_kernel,
        in_specs=[vmem] * 3,
        out_specs=[vmem] * 2,
        out_shape=[jax.ShapeDtypeStruct(across.shape, BF16)] * 2,
        compiler_params=params(),
        name="packed",
    )(own, beside, across)


def turn(second, k, spans, local, out):
    me = lax.axis_index("feat")
    width = second.shape[2]
    for h in range(2):
        rows = []
        for relative, source, start, half in spans:
            if relative:
                at = pl.multiple_of((me ^ source) * local + start + h * half, 8)
            else:
                at = source * local + start + h * half
            rows.append(second[k, pl.ds(at, half), :])
        depth = out.shape[2] // 2
        out[k, :, h * depth : (h + 1) * depth] = jnp.concatenate(rows, axis=0).T


def products(k, factors, pieces, rows):
    total = None
    for a, own in zip(factors, pieces):
        groups = a.shape[0]
        right = jnp.concatenate([x[at + k] for x in own for at in range(0, x.shape[0], groups)], axis=0)
        right = jnp.concatenate([right[:, :rows], right[:, rows:]], axis=0)
        part = lax.dot_general(a[k], right, NN, preferred_element_type=F32)
        total = part if total is None else total + part
    return total.T


def early_kernel(plan, local, counts, second, *refs):
    refs = list(refs)
    pieces = [[refs.pop(0) for _ in range(n)] for n in counts]
    out, late, held, sem, *factors = refs
    copy = pltpu.make_async_copy(second, held, sem)
    copy.start()
    copy.wait()
    groups, _, width = held.shape
    for k in range(groups):
        for spans, factor in zip(plan, factors + [late]):
            turn(held, k, spans, local, factor)
        out[:, k * width : (k + 1) * width] = products(k, factors, pieces, out.shape[0])


def early_products(second, plan, local, pieces, rows):
    groups, _, width = second.shape
    vmem = pl.BlockSpec(memory_space=pltpu.VMEM)
    counts = [len(own) for own in pieces]
    shapes = [(groups, width, 2 * sum(span[-1] for span in spans)) for spans in plan]
    return pl.pallas_call(
        functools.partial(early_kernel, plan, local, counts),
        in_specs=[pl.BlockSpec(memory_space=pl.ANY)] + [vmem] * sum(counts),
        out_specs=[vmem] * 2,
        out_shape=[jax.ShapeDtypeStruct((rows, groups * width), F32), jax.ShapeDtypeStruct(shapes[-1], BF16)],
        scratch_shapes=[pltpu.VMEM(second.shape, BF16), pltpu.SemaphoreType.DMA]
        + [pltpu.VMEM(shape, BF16) for shape in shapes[:-1]],
        compiler_params=params(),
        cost_estimate=pl.CostEstimate(flops=2000000000, bytes_accessed=2000000, transcendentals=0),
        name="early_products",
    )(second, *[x for own in pieces for x in own])


def late_kernel(picks, early, factor, *refs):
    *pieces, sketch, mine, other, held = refs
    groups, width, _ = factor.shape
    rows = sketch.shape[0]
    slots = mine.shape[1]
    if groups < slots:
        held[...] = jnp.zeros_like(held)
    for k in range(groups):
        cols = slice(k * width, (k + 1) * width)
        mapped = early[:, cols] + products(k, [factor], [pieces], rows)
        sketch[:, cols] = mapped
        held[pl.ds(k, rows, stride=slots), :] = mapped
    rounds, each = picks.shape
    place = lax.axis_index("ex")
    base, core = place * rows, place % 2
    half = rounds // 2
    for r in range(half):
        for p in range(each):
            for out, side in ((mine, core), (other, 1 - core)):
                at = picks[side * half + r, p] - base
                held_here = (at >= 0) & (at < rows)
                start = pl.multiple_of(jnp.clip(at, 0, rows - 1) * slots, slots)
                out[r * each + p] = jnp.where(held_here, held[pl.ds(start, slots), :], 0.0)


def late_products(picks, early, factor, pieces):
    rows = early.shape[0]
    groups, width, _ = factor.shape
    slots = -(-groups // 8) * 8
    smem = pl.BlockSpec(memory_space=pltpu.SMEM)
    vmem = pl.BlockSpec(memory_space=pltpu.VMEM)
    fetched = jax.ShapeDtypeStruct((picks.size // 2, slots, width), F32)
    return pl.pallas_call(
        late_kernel,
        in_specs=[smem] + [vmem] * (2 + len(pieces)),
        out_specs=[vmem] * 3,
        out_shape=[jax.ShapeDtypeStruct(early.shape, F32), fetched, fetched],
        scratch_shapes=[pltpu.VMEM((rows * slots, width), F32)],
        compiler_params=params(),
        name="late_products",
    )(picks, early, factor, *pieces)


def distance_kernel(unroll, sketch, first, second, *refs):
    if len(refs) == 4:
        kept, out, center, sem = refs
        before = None
        copy = pltpu.make_async_copy(sketch, kept, sem)
        copy.start()
    else:
        before, out, center = refs
        copy = None
    rows, dims = sketch.shape
    count, _, width = center.shape
    center[...] = first[...] + second[...]
    lane = lax.broadcasted_iota(jnp.int32, (8, 128), 1)
    sums = [jnp.zeros((8, 128), F32)] * (rows // 8)
    for p in range(0, count, unroll):
        for g in range(rows // 8):
            block = [sketch[g * 8 : (g + 1) * 8, t * width : (t + 1) * width] for t in range(dims // width)]
            for u in range(unroll):
                acc = None
                for t, own in enumerate(block):
                    diff = own - center[p + u, t : t + 1, :]
                    acc = diff * diff if acc is None else acc + diff * diff
                sums[g] = jnp.where(lane == p + u, jnp.sum(acc, axis=1, keepdims=True), sums[g])
    by_pick = jnp.concatenate(sums, axis=0).T[:count]
    if before is not None:
        by_pick = jnp.concatenate([before[...], by_pick], axis=1)
    out[...] = by_pick.astype(out.dtype)
    if copy is not None:
        copy.wait()


def distances(sketch, first, second, before=None):
    vmem = pl.BlockSpec(memory_space=pltpu.VMEM)
    hbm = pl.BlockSpec(memory_space=pl.ANY)
    count, rows = first.shape[0], sketch.shape[0]
    center = pltpu.VMEM(first.shape, F32)
    if before is None:
        return pl.pallas_call(
            functools.partial(distance_kernel, 4),
            in_specs=[vmem] * 3,
            out_specs=[hbm, vmem],
            out_shape=[jax.ShapeDtypeStruct(sketch.shape, F32), jax.ShapeDtypeStruct((count, rows), F32)],
            scratch_shapes=[center, pltpu.SemaphoreType.DMA],
            compiler_params=params(),
            name="distances",
        )(sketch, first, second)
    return pl.pallas_call(
        functools.partial(distance_kernel, 4),
        in_specs=[vmem] * 4,
        out_specs=vmem,
        out_shape=jax.ShapeDtypeStruct((count, 2 * rows), BF16),
        scratch_shapes=[center],
        compiler_params=params(),
        name="distances",
    )(sketch, first, second, before)


def nearest_kernel(sketch_size, each, parts, out):
    total = parts[0].astype(F32)
    for i in range(1, parts.shape[0]):
        total = total + parts[i].astype(F32)
    total = total / sketch_size
    half, rows = out.shape[0] // 2, out.shape[1]
    core = lax.axis_index("ex") % 2
    near = [jnp.min(total[r * each : (r + 1) * each, :], axis=0, keepdims=True) for r in range(half)]
    running = None
    for r in range(2 * half):
        own, other = near[r % half][:, :rows], near[r % half][:, rows:]
        row = jnp.where(core == r // half, own, other)
        running = row if running is None else jnp.minimum(running, row)
        out[r : r + 1, :] = running


def nearest(parts, sketch_size, rounds):
    vmem = pl.BlockSpec(memory_space=pltpu.VMEM)
    each = 2 * parts.shape[1] // rounds
    return pl.pallas_call(
        functools.partial(nearest_kernel, sketch_size, each),
        in_specs=[vmem],
        out_specs=vmem,
        out_shape=jax.ShapeDtypeStruct((rounds, parts.shape[2] // 2), F32),
        compiler_params=params(),
        name="nearest",
    )(parts)


def swap(x, axis, size, step):
    return lax.ppermute(x, axis, [(i, i ^ step) for i in range(size)])


def per_device(feat, ex, grads, first_factor, second_factor, picks):
    rows = grads.shape[0]
    local = first_factor.shape[0]
    groups, _, width = second_factor.shape
    near = feat // 2
    factor = jnp.swapaxes(first_factor, 1, 2)
    count = local // 2 if local % 64 == 0 else local
    start, half = local - count, count // 2
    pieces, plan = [], []
    if start:
        (inner,) = first_products(grads, factor, feat, False, False, 0, start)
        pieces.append([lax.all_to_all(inner, "feat", split_axis=0, concat_axis=0, tiled=True)])
        plan.append([(False, d, 0, start // 2) for d in range(feat)])
    pair = near == 4
    split = first_products(grads, factor, feat, pair, True, start, count)
    far = [swap(x, "feat", feat, near + i) for i, x in enumerate(split[len(split) - near :])]
    far_places = list(range(near, feat))
    if pair:
        across = swap(split[2], "feat", feat, 2)
        close, message = packed(split[0], split[1], across)
        close, near_places = [close], [0, 2]
        far, far_places = far + [swap(message, "feat", feat, 1)], far_places + [1, 3]
    else:
        close = [x if d == 0 else swap(x, "feat", feat, d) for d, x in enumerate(split[:near])]
        near_places = list(range(near))
    pieces += [close, far]
    plan += [[(True, d, start, half) for d in places] for places in (near_places, far_places)]

    early, turned = early_products(second_factor, plan, local, pieces[:-1], rows)
    sketch, mine, other = late_products(picks, early, turned, pieces[-1])

    chip = mine + swap(other, "ex", ex, 1)
    across = [chip]
    step = 2
    while step < ex:
        across = across + [swap(x, "ex", ex, step) for x in across]
        step *= 2
    across = [across[0], sum(across[1:])]
    kept, part = distances(sketch, *across)
    part = distances(sketch, *[swap(x, "ex", ex, 1) for x in across], before=part)
    spread = jnp.broadcast_to(part[None], (feat,) + part.shape)
    gathered = lax.all_to_all(spread, "feat", split_axis=0, concat_axis=0, tiled=True)
    coverage = nearest(gathered, feat * groups * width, picks.shape[0])
    return (kept, coverage)


def solution(mesh):
    feat, ex = mesh.shape["feat"], mesh.shape["ex"]
    in_specs = (P("ex", "feat"), P("feat", None, None), P("feat", None, None), P())
    out_specs = (P("ex", "feat"), P(None, "ex"))
    return jax.shard_map(
        functools.partial(per_device, feat, ex),
        mesh=mesh,
        in_specs=in_specs,
        out_specs=out_specs,
        check_vma=False,
    )
```
